256 devices in a mesh: row: 16 (over y, x), col: 16 (over z, core).
Axes of the slice: x: 4, y: 4, z: 8, core: 2. Of those that a mesh axis runs over, the one named last changes fastest.
Arguments:
- xblocks: bfloat16 [128, 32, 128, 128], P('row', 'col'), may hold values from -0.109375 to 0.109375
- reach: int32 [128, 2], P('row'), may hold values from 3 to 11, as said below
Outputs:
- new_x: bfloat16 [128, 32, 128, 128], P('row', 'col')
- row_error: float32 [128], P('row')
The draws below stay inside these ranges and needn't reach their ends.
Inputs may be any that keep to these rules, and one draw needn't show every extreme that they name: `reach`: some stored block row reaches 11 blocks on both sides.
All inputs are finite; a program needn't handle non-finite values.
Results may differ from the reference program's by a relative error of at most 0.0017.
Values may be sent and summed in bfloat16 or wider, within the bound.
No kernel may reach another device: no remote copies, remote signals or barrier semaphores. Data moves between devices by JAX's collectives and lax.ppermute only.
A program may use at most 128 MiB of HBM per device.

```python
import jax
import jax.numpy as jnp
from jax import lax

BS = 128
H = 11
BR = 8
NB = 128
W = 2
SLOTS = 32
N_ROW = 16
N_COL = 16


def draw_reach(key, part):
    key = jax.random.fold_in(key, 11)
    first_key, second_key = jax.random.split(key)
    values = jax.random.randint(first_key, (NB, 2), H // 3, H + 1, dtype=jnp.int32)
    chosen = jax.random.randint(second_key, (), 0, NB, dtype=jnp.int32)
    full_row = jnp.arange(NB, dtype=jnp.int32) == chosen
    return jnp.where(full_row[:, None], jnp.int32(H), values).astype(jnp.int32)


def level_of(stream_key, dims, pieces, least, high):
    factor_of, own = 1.0, jax.random.fold_in(stream_key, 6)
    for position, blocks in pieces:
        heights = jnp.exp(jax.random.uniform(jax.random.fold_in(own, position), (blocks,), jnp.float32, least / len(pieces), high / len(pieces)))
        factor_of = factor_of * jnp.repeat(heights, dims[position] // blocks).reshape([-1 if axis == position else 1 for axis in range(len(dims))])
    return factor_of


def centred(rng, shape, spread, limit, cuts=(), kind=jnp.bfloat16):
    entries = spread * jax.random.normal(rng, shape, jnp.float32)
    if cuts:
        entries = entries * level_of(rng, shape, cuts, -0.22, 0.18)
    return jnp.clip(entries, -limit, limit).astype(kind)


def setup_inputs(seed: int = 0) -> dict:
    key_of = jax.random.split(jax.random.key(seed), 3)
    return {
        "xblocks": centred(key_of[0], (NB, SLOTS, BS, BS), (BS * (2 * H + 1)) ** -0.5, 0.109375, ((0, 16), (1, 16))),
        "reach": draw_reach(jax.random.fold_in(key_of[2], 71), 0),
    }


def band_layout(reach):
    row_ids = jnp.arange(NB, dtype=jnp.int32)
    offsets = jnp.arange(2 * H + 1, dtype=jnp.int32) - H
    stored = row_ids % N_ROW * BR + row_ids // N_ROW
    columns = (row_ids[:, None] + offsets[None, :]) % NB
    tile_ids = columns % N_COL
    first_offset = (tile_ids - row_ids[:, None] + H) % N_COL - H
    slot_ids = tile_ids * W + (offsets[None, :] - first_offset) // N_COL
    low_reach = reach[stored, 0]
    high_reach = reach[stored, 1]
    live_mask = (offsets[None, :] >= -low_reach[:, None]) & (offsets[None, :] <= high_reach[:, None])
    return (stored, slot_ids, live_mask)

def band_product(left_band, right_band, live_mask):
    span = 2 * H + 1
    offsets = jnp.arange(span, dtype=jnp.int32) - H
    shift_index = (offsets[None, :] - offsets[:, None] + H) % NB
    inside = shift_index < span
    clipped = jnp.clip(shift_index, 0, span - 1)

    def one_row(row_id):
        key_rows = (row_id + offsets) % NB
        picked = right_band[key_rows[:, None], clipped].astype(jnp.float32)
        picked = jnp.where(inside[:, :, None, None], picked, jnp.zeros((), jnp.float32))
        return jnp.einsum('eij,edjk->dik', left_band[row_id].astype(jnp.float32), picked)
    result = lax.map(one_row, jnp.arange(NB, dtype=jnp.int32))
    return jnp.where(live_mask[:, :, None, None], result, jnp.zeros((), jnp.float32))

def reference(xblocks, reach):
    stored, slot_ids, live_mask = band_layout(reach)
    banded = xblocks[stored[:, None], slot_ids]
    banded = jnp.where(live_mask[:, :, None, None], banded, jnp.zeros((), xblocks.dtype))
    square_f = band_product(banded, banded, live_mask)
    offsets = jnp.arange(2 * H + 1, dtype=jnp.int32) - H
    centre = (offsets == 0).astype(jnp.float32)
    identity = jnp.eye(BS, dtype=jnp.float32)
    deviation = square_f - centre[None, :, None, None] * identity
    deviation = jnp.where(live_mask[:, :, None, None], deviation, jnp.zeros((), jnp.float32))
    logical_error = jnp.sqrt(lax.optimization_barrier(jnp.sum(deviation * deviation, axis=(1, 2, 3))) / BS)
    square_b = square_f.astype(jnp.bfloat16)
    cube_term = band_product(banded, square_b, live_mask)
    updated = (1.5 * banded.astype(jnp.float32) - 0.5 * cube_term).astype(jnp.bfloat16)
    stored_ids = jnp.arange(NB, dtype=jnp.int32)
    logical_ids = stored_ids % BR * N_ROW + stored_ids // BR
    slot_all = jnp.arange(SLOTS, dtype=jnp.int32)
    offset_all = (slot_all[None, :] // W - logical_ids[:, None] + H) % N_COL - H + N_COL * (slot_all[None, :] % W)
    keep = (offset_all >= -reach[:, 0:1]) & (offset_all <= reach[:, 1:2])
    new_x = updated[logical_ids[:, None], jnp.clip(offset_all + H, 0, 2 * H)]
    new_x = jnp.where(keep[:, :, None, None], new_x, jnp.zeros((), jnp.bfloat16))
    return (new_x, logical_error[logical_ids])
```

```python
import jax
import jax.numpy as jnp
from jax import lax
from jax.experimental import pallas as pl
from jax.experimental.pallas import tpu as pltpu
from jax.sharding import PartitionSpec as P

H = 11
UNROLL = 4
SHIFTS = (0, -1, 1, 2)


def band_offset(tile_id, logical, col_count, slot_index):
    return (tile_id - logical + H) % col_count - H + col_count * slot_index


def core_pairs(step, phase):
    pairs = []
    for y in range(4):
        for x in range(4):
            for col in range(16):
                if col % 2 == phase:
                    target = y * 4 + (x + step) % 4
                else:
                    target = (y + step) % 4 * 4 + x
                pairs.append(((y * 4 + x) * 16 + col, target * 16 + col))
    return pairs


def row_panel(shard):
    def move(value, step, phase):
        return lax.ppermute(value, ("row", "col"), core_pairs(step, phase))

    def spread(value, phase):
        return [move(value, 1, phase), move(value, -1, phase), move(value, 2, phase)]

    group = jnp.concatenate([shard] + spread(shard, 0), axis=0)
    return [group] + spread(group, 1)


def band_kernel(
    squaring, place, reach, left, right0, right1, right2, right3, own, out, err, lv, wv, lsem, wsem
):
    a = place[0]
    b = place[1]
    core = b % 2
    x = a % 4
    y = a // 4
    u = jnp.where(core == 0, x, y)
    v = jnp.where(core == 0, y, x)
    copies = []
    for m, source in enumerate((right0, right1, right2, right3)):
        for j in range(4):
            uu = (u + SHIFTS[j] + 4) % 4
            vv = (v + SHIFTS[m] + 4) % 4
            origin = jnp.where(core == 0, 4 * vv + uu, 4 * uu + vv)
            copies.append(
                pltpu.make_async_copy(source.at[pl.ds(8 * j, 8)], wv.at[origin], wsem.at[m * 4 + j])
            )
    rows = [pltpu.make_async_copy(left.at[:, i], lv.at[i], lsem.at[i]) for i in range(8)]
    for copy in copies + rows:
        copy.start()
    for copy in copies:
        copy.wait()
    eye = (
        lax.broadcasted_iota(jnp.int32, (128, 128), 0)
        == lax.broadcasted_iota(jnp.int32, (128, 128), 1)
    ).astype(jnp.float32)
    first = (b - a + H + 16) % 16 - H
    for i in range(8):
        rows[i].wait()
        low = reach[i, 0]
        high = reach[i, 1]
        r = a + 16 * i
        row_err = jnp.zeros((1, 128), jnp.float32)
        for w in range(2):
            target = first + 16 * w
            live = (target >= -low) & (target <= high)
            begin = jnp.maximum(target - H, -low)
            end = jnp.minimum(target + H, high)
            steps = jnp.where(live, (end - begin + UNROLL) // UNROLL, 0)

            def body(n, acc):
                lefts, rights = [], []
                for q in range(UNROLL):
                    d = begin + n * UNROLL + q
                    inside = d <= end
                    d = jnp.minimum(d, end)
                    k = r + d + 128
                    block = lv[i, k % 16, (d + H) // 16]
                    lefts.append(jnp.where(inside, block, jnp.zeros_like(block)))
                    rights.append(wv[k % 16, k // 16 % 8, (target - d + H) // 16])
                return acc + jnp.dot(
                    jnp.concatenate(lefts, axis=1),
                    jnp.concatenate(rights, axis=0),
                    preferred_element_type=jnp.float32,
                )

            acc = lax.fori_loop(0, steps, body, jnp.zeros((128, 128), jnp.float32))
            if squaring:
                centre = jnp.where(live & (target == 0), 1.0, 0.0)
                deviation = acc - centre * eye
                row_err = row_err + jnp.sum(deviation * deviation, axis=0, keepdims=True)
                out[i, w] = acc.astype(jnp.bfloat16)
            else:
                mine = jnp.where(live, own[i, w].astype(jnp.float32), 0.0)
                out[i, w] = (1.5 * mine - 0.5 * acc).astype(jnp.bfloat16)
        err[pl.ds(i, 1), :] = row_err


def band_product(squaring, place, reach, left, right, own):
    import functools

    smem = pl.BlockSpec(memory_space=pltpu.SMEM)
    vmem = pl.BlockSpec(memory_space=pltpu.VMEM)
    anywhere = pl.BlockSpec(memory_space=pl.ANY)
    return pl.pallas_call(
        functools.partial(band_kernel, squaring),
        out_shape=(
            jax.ShapeDtypeStruct(own.shape, jnp.bfloat16),
            jax.ShapeDtypeStruct((8, 128), jnp.float32),
        ),
        in_specs=[smem, smem] + [anywhere] * 5 + [vmem],
        out_specs=(vmem, vmem),
        scratch_shapes=[
            pltpu.VMEM((8, 16, 2, 128, 128), jnp.bfloat16),
            pltpu.VMEM((16, 8, 2, 128, 128), jnp.bfloat16),
            pltpu.SemaphoreType.DMA((8,)),
            pltpu.SemaphoreType.DMA((16,)),
        ],
        compiler_params=pltpu.CompilerParams(vmem_limit_bytes=40 * 1024 * 1024),
        cost_estimate=pl.CostEstimate(
            flops=10**9, bytes_accessed=17 * 2**20, transcendentals=0
        ),
        name="square" if squaring else "cube",
    )(place, reach, left, *right, own)


def per_device(xblocks, reach):
    row_pos = lax.axis_index("row")
    col_pos = lax.axis_index("col")
    logical = jnp.arange(8, dtype=jnp.int32) * 16 + row_pos
    slots = jnp.arange(2, dtype=jnp.int32)
    own_offset = band_offset(col_pos, logical[:, None], 16, slots[None, :])
    live_mask = (own_offset >= -reach[:, 0:1]) & (own_offset <= reach[:, 1:2])
    place = jnp.stack([row_pos, col_pos]).astype(jnp.int32)

    left = lax.all_gather(xblocks, "col", axis=0)
    masked = jnp.where(live_mask[:, :, None, None], xblocks, jnp.zeros((), xblocks.dtype))
    square, partial_sq = band_product(True, place, reach, left, row_panel(masked), xblocks)
    wide = jnp.broadcast_to(partial_sq[None], (16, 8, 128))
    spread = lax.all_gather(wide, "col", axis=0)
    row_error = jnp.sqrt(jnp.sum(spread[:, 0], axis=(0, 2)) / 128)
    new_x, _ = band_product(False, place, reach, left, row_panel(square), xblocks)
    return (new_x, row_error)


def solution(mesh):
    placed = (P("row", "col", None, None), P("row", None))
    return jax.shard_map(
        per_device,
        mesh=mesh,
        in_specs=placed,
        out_specs=(P("row", "col", None, None), P("row")),
        check_vma=False,
    )
```

```python
import functools

import jax
import jax.numpy as jnp
from jax import lax
from jax.experimental import pallas as pl
from jax.experimental.pallas import tpu as pltpu
from jax.sharding import PartitionSpec as P

H = 11
SHIFTS = (0, -1, 1, 2)
OPPOSITE = (3, 2, 1, 0)
BLOCK = (128, 128)


def core_pairs(step, phase):
    pairs = []
    for y in range(4):
        for x in range(4):
            for col in range(16):
                if col % 2 == phase:
                    target = y * 4 + (x + step) % 4
                else:
                    target = (y + step) % 4 * 4 + x
                pairs.append(((y * 4 + x) * 16 + col, target * 16 + col))
    return pairs


def move(value, pairs):
    return lax.ppermute(value, ("row", "col"), pairs)


def half_way(value):
    pairs = [(r * 16 + c, (r + 8) % 16 * 16 + c) for r in range(16) for c in range(16)]
    return move(value, pairs)


def spread(value, phase):
    return [move(value, core_pairs(step, phase)) for step in (1, -1, 2)]


def panel_of(shard):
    near = spread(shard, 0)
    other = move(near[0][0, :16], [(n, n ^ 1) for n in range(256)])
    arrived = jnp.abs(other[0, 0].astype(jnp.float32)) < 3e38
    near[0] = jnp.where(arrived, near[0], jnp.zeros((), near[0].dtype))
    group = jnp.stack([shard] + near, axis=0)
    return [group] + spread(group, 1)


def wrap(offset):
    return ((offset + H + 16) & 15) - H


class Where:
    def __init__(self, place):
        self.a = place[0]
        self.b = place[1]
        self.x_major = (self.b & 1) == 0
        x = self.a & 3
        y = self.a >> 2
        self.u = jnp.where(self.x_major, x, y)
        self.v = jnp.where(self.x_major, y, x)
        self.first = wrap(self.b - self.a)

    def origin(self, m, j):
        uu = (self.u + SHIFTS[j] + 4) & 3
        vv = (self.v + SHIFTS[m] + 4) & 3
        return jnp.where(self.x_major, 4 * vv + uu, 4 * uu + vv)

    def two_slots(self, origin):
        return wrap(self.b - origin) + 16 <= H


def gather_second(where, groups, pieces, seconds, sems):
    order = [(m, j) for m in groups for j in range(4)]
    copies = []
    for n, (m, j) in enumerate(order):
        partner = jnp.where(
            where.x_major, order.index((OPPOSITE[m], j)), order.index((m, OPPOSITE[j]))
        )
        target = jnp.where(where.two_slots(where.origin(m, j)), n * 8, partner * 8 + 4)
        copies.append(
            pltpu.make_async_copy(
                pieces[groups.index(m)].at[j, pl.ds(8, 4)], seconds.at[pl.ds(target, 4)], sems.at[n]
            )
        )
        copies[-1].start()
    seconds[seconds.shape[0] - 1] = jnp.zeros(BLOCK, jnp.bfloat16)
    return copies


def row_sum(where, groups, row, low, high, pieces, seconds, panel, acc):
    none = seconds.shape[0] - 1
    absent = 32

    def left_block(origin, offset):
        held = (offset >= -low) & (offset <= high)
        return panel[jnp.where(held, 2 * origin + ((offset + H) >> 4), absent)]

    for n, (m, j) in enumerate((m, j) for m in groups for j in range(4)):
        piece = pieces[groups.index(m)]
        origin = where.origin(m, j)
        offset = where.first - wrap(where.b - origin)
        two = where.two_slots(origin)
        ahead = offset >= 5
        k0 = ((where.a + 16 * row + offset + 128) >> 4) & 7
        k1 = jnp.where(ahead, k0 + 7, k0 + 1) & 7
        q00 = piece[j, k0]
        q01 = seconds[jnp.where(two, n * 8 + k0, none)]
        q10 = seconds[jnp.where(two & ahead, n * 8 + k1, none)]
        q11 = piece[j, k1] * jnp.where(ahead, 0.0, 1.0).astype(jnp.bfloat16)
        acc += jnp.dot(
            jnp.concatenate(
                [
                    left_block(origin, offset),
                    left_block(origin, jnp.where(ahead, offset - 16, offset + 16)),
                ],
                axis=1,
            ),
            jnp.concatenate(
                [jnp.concatenate([q00, q01], axis=1), jnp.concatenate([q10, q11], axis=1)], axis=0
            ),
            preferred_element_type=jnp.float32,
        )
    return acc


def load_rows(start, count, left, panel, sems):
    copies = [
        pltpu.make_async_copy(left.at[:, start + i], panel.at[i, pl.ds(0, 16)], sems.at[i])
        for i in range(count)
    ]
    for copy in copies:
        copy.start()
    return copies


def product_rows(start, count, groups, place, reach, left, pieces, scratch, initial, finish):
    seconds, panel, sems, row_sems = scratch
    where = Where(place)
    copies = gather_second(where, groups, pieces, seconds, sems)
    rows = load_rows(start, count, left, panel, row_sems)
    for i in range(count):
        panel[i, 16, 0] = jnp.zeros(BLOCK, jnp.bfloat16)
    for copy in copies:
        copy.wait()
    for i in range(count):
        rows[i].wait()
        low = reach[start + i, 0]
        high = reach[start + i, 1]
        flat = panel.at[i].reshape(34, 128, 128)
        acc = row_sum(where, groups, start + i, low, high, pieces, seconds, flat, initial(i))
        live0 = (where.first >= -low) & (where.first <= high)
        live1 = where.first + 16 <= high
        finish(where, i, acc, live0, live1)


def no_sum(i):
    return jnp.zeros((128, 256), jnp.float32)


def square_kernel(start, count, groups, place, reach, left, *refs):
    pieces, (first, second, err), scratch = refs[:4], refs[4:7], refs[7:]
    eye = (
        lax.broadcasted_iota(jnp.int32, BLOCK, 0) == lax.broadcasted_iota(jnp.int32, BLOCK, 1)
    ).astype(jnp.float32)

    def finish(where, i, acc, live0, live1):
        total0 = jnp.where(live0, acc[:, :128], 0.0)
        total1 = jnp.where(live1, acc[:, 128:], 0.0)
        first[i] = total0.astype(jnp.bfloat16)
        second[i] = total1.astype(jnp.bfloat16)
        deviation = total0 - jnp.where(live0 & (where.first == 0), 1.0, 0.0) * eye
        squares = deviation * deviation + total1 * total1
        err[i] = jnp.sum(squares.reshape(16, 8, 128), axis=0)

    product_rows(start, count, groups, place, reach, left, pieces, scratch, no_sum, finish)


def early_kernel(groups, place, reach, left, *refs):
    pieces, out, scratch = refs[:2], refs[2], refs[3:]

    def finish(where, i, acc, live0, live1):
        out[i] = acc

    product_rows(0, 8, groups, place, reach, left, pieces, scratch, no_sum, finish)


def late_kernel(groups, place, reach, left, early, own, *refs):
    pieces, out, scratch = refs[:2], refs[2], refs[3:]

    def finish(where, i, acc, live0, live1):
        for w, live in enumerate((live0, live1)):
            updated = 1.5 * own[i, w].astype(jnp.float32) - 0.5 * acc[:, 128 * w : 128 * w + 128]
            out[i, w] = jnp.where(live, updated, 0.0).astype(jnp.bfloat16)

    product_rows(0, 8, groups, place, reach, left, pieces, scratch, lambda i: early[i], finish)


SMEM = pl.BlockSpec(memory_space=pltpu.SMEM)
VMEM = pl.BlockSpec(memory_space=pltpu.VMEM)
ANY = pl.BlockSpec(memory_space=pl.ANY)


def call(kernel, name, outs, count, groups, args):
    steps = 4 * count * len(groups)
    return pl.pallas_call(
        functools.partial(kernel, groups),
        out_shape=outs,
        in_specs=[SMEM, SMEM, ANY] + [VMEM] * (len(args) - 3),
        out_specs=jax.tree.map(lambda _: VMEM, outs),
        scratch_shapes=[
            pltpu.VMEM((32 * len(groups) + 1, 128, 128), jnp.bfloat16),
            pltpu.VMEM((count, 17, 2, 128, 128), jnp.bfloat16),
            pltpu.SemaphoreType.DMA((4 * len(groups),)),
            pltpu.SemaphoreType.DMA((count,)),
        ],
        compiler_params=pltpu.CompilerParams(vmem_limit_bytes=50 * 2**20),
        cost_estimate=pl.CostEstimate(
            flops=steps * 2**24, bytes_accessed=steps * 2**16, transcendentals=0
        ),
        name=name,
    )(*args)


def bf16(*shape):
    return jax.ShapeDtypeStruct(shape, jnp.bfloat16)


def f32(*shape):
    return jax.ShapeDtypeStruct(shape, jnp.float32)


def square_rows(start, args):
    return call(
        lambda groups, *refs: square_kernel(start, 4, groups, *refs),
        "square",
        (bf16(4, 128, 128), bf16(4, 128, 128), f32(4, 8, 128)),
        4,
        (0, 1, 2, 3),
        args,
    )


def per_device(xblocks, reach):
    row_pos = lax.axis_index("row")
    col_pos = lax.axis_index("col")
    place = jnp.stack([row_pos, col_pos]).astype(jnp.int32)
    offset = (col_pos - row_pos + H) % 16 - H
    two_slots = offset + 16 <= H
    own_offset = offset + 16 * jnp.arange(2, dtype=jnp.int32)[None, :]
    live_mask = (own_offset >= -reach[:, 0:1]) & (own_offset <= reach[:, 1:2])

    left = lax.all_gather(xblocks, "col", axis=0)
    masked = jnp.where(live_mask[:, :, None, None], xblocks, jnp.zeros((), xblocks.dtype))
    other = half_way(masked[4:, 1])
    shard = jnp.concatenate([masked[:, 0], jnp.where(two_slots, masked[:4, 1], other)], axis=0)
    panel = panel_of(shard)
    upper = square_rows(4, (place, reach, left, *panel))
    other = half_way(upper[1])
    lower = square_rows(0, (place, reach, left, *panel))
    second = jnp.where(two_slots, lower[1], other)
    panel = panel_of(jnp.concatenate([lower[0], upper[0], second], axis=0))

    parts = jnp.concatenate([lower[2], upper[2]], axis=0)
    parts = lax.all_gather(jnp.sum(parts, axis=1), "col", axis=0)
    row_error = jnp.sqrt(jnp.sum(parts, axis=(0, 2)) / 128)

    early = call(
        early_kernel, "early", f32(8, 128, 256), 8, (0, 3), (place, reach, left, panel[0], panel[3])
    )
    new_x = call(
        late_kernel,
        "late",
        bf16(8, 2, 128, 128),
        8,
        (1, 2),
        (place, reach, left, early, xblocks, panel[1], panel[2]),
    )
    return (new_x, row_error)


def solution(mesh):
    placed = (P("row", "col", None, None), P("row", None))
    return jax.shard_map(
        per_device,
        mesh=mesh,
        in_specs=placed,
        out_specs=(P("row", "col", None, None), P("row")),
        check_vma=False,
    )
```

```python
import functools

import jax
import jax.numpy as jnp
from jax import lax
from jax.experimental import pallas as pl
from jax.experimental.pallas import tpu as pltpu
from jax.sharding import PartitionSpec as P

H = 11
SHIFTS = (0, -1, 1, 2)
OPPOSITE = (3, 2, 1, 0)
BLOCK = (128, 128)


def core_pairs(step, phase):
    pairs = []
    for y in range(4):
        for x in range(4):
            for col in range(16):
                if col % 2 == phase:
                    target = y * 4 + (x + step) % 4
                else:
                    target = (y + step) % 4 * 4 + x
                pairs.append(((y * 4 + x) * 16 + col, target * 16 + col))
    return pairs


def move(value, pairs):
    return lax.ppermute(value, ("row", "col"), pairs)


def half_way(value):
    pairs = [(r * 16 + c, (r + 8) % 16 * 16 + c) for r in range(16) for c in range(16)]
    return move(value, pairs)


def spread(value, phase):
    return [move(value, core_pairs(step, phase)) for step in (1, -1, 2)]


def panel_of(shard):
    near = spread(shard, 0)
    other = move(near[0][0, :16], [(n, n ^ 1) for n in range(256)])
    arrived = jnp.abs(other[0, 0].astype(jnp.float32)) < 3e38
    near[0] = jnp.where(arrived, near[0], jnp.zeros((), near[0].dtype))
    halves = [jnp.stack([shard, near[0]], axis=0), jnp.stack(near[1:], axis=0)]
    before = [move(half, core_pairs(1, 1)) for half in halves]
    after = [move(half, core_pairs(-1, 1)) for half in halves]
    passed = [move(before[0], core_pairs(1, 1)), move(after[1], core_pairs(-1, 1))]
    return [halves, before, after, passed]


def wrap(offset):
    return ((offset + H + 16) & 15) - H


class Where:
    def __init__(self, place):
        self.a = place[0]
        self.b = place[1]
        self.x_major = (self.b & 1) == 0
        x = self.a & 3
        y = self.a >> 2
        self.u = jnp.where(self.x_major, x, y)
        self.v = jnp.where(self.x_major, y, x)
        self.first = wrap(self.b - self.a)

    def origin(self, m, j):
        uu = (self.u + SHIFTS[j] + 4) & 3
        vv = (self.v + SHIFTS[m] + 4) & 3
        return jnp.where(self.x_major, 4 * vv + uu, 4 * uu + vv)

    def two_slots(self, origin):
        return wrap(self.b - origin) + 16 <= H


def gather_second(where, groups, pieces, seconds):
    order = [(m, j) for m in groups for j in range(4)]
    for n, (m, j) in enumerate(order):
        partner = jnp.where(
            where.x_major, order.index((OPPOSITE[m], j)), order.index((m, OPPOSITE[j]))
        )
        target = jnp.where(where.two_slots(where.origin(m, j)), n * 8, partner * 8 + 4)
        for k in range(4):
            seconds[target + k] = pieces[groups.index(m)][j // 2][j % 2, 8 + k]
    seconds[seconds.shape[0] - 1] = jnp.zeros(BLOCK, jnp.bfloat16)


def row_sum(where, groups, row, low, high, pieces, seconds, panel, acc):
    none = seconds.shape[0] - 1
    absent = 32

    def left_block(origin, offset):
        held = (offset >= -low) & (offset <= high)
        return panel[jnp.where(held, 2 * origin + ((offset + H) >> 4), absent)]

    for n, (m, j) in enumerate((m, j) for m in groups for j in range(4)):
        piece = pieces[groups.index(m)][j // 2].at[j % 2]
        origin = where.origin(m, j)
        offset = where.first - wrap(where.b - origin)
        two = where.two_slots(origin)
        ahead = offset >= 5
        k0 = ((where.a + 16 * row + offset + 128) >> 4) & 7
        k1 = jnp.where(ahead, k0 + 7, k0 + 1) & 7
        q00 = piece[k0]
        q01 = seconds[jnp.where(two, n * 8 + k0, none)]
        q10 = seconds[jnp.where(two & ahead, n * 8 + k1, none)]
        q11 = piece[k1] * jnp.where(ahead, 0.0, 1.0).astype(jnp.bfloat16)
        acc += jnp.dot(
            jnp.concatenate(
                [
                    left_block(origin, offset),
                    left_block(origin, jnp.where(ahead, offset - 16, offset + 16)),
                ],
                axis=1,
            ),
            jnp.concatenate(
                [jnp.concatenate([q00, q01], axis=1), jnp.concatenate([q10, q11], axis=1)], axis=0
            ),
            preferred_element_type=jnp.float32,
        )
    return acc


def row_copies(start, count, left, panel, sems):
    return [
        pltpu.make_async_copy(left.at[:, start + i], panel.at[i, pl.ds(0, 16)], sems.at[i])
        for i in range(count)
    ]


def product_rows(start, count, groups, place, reach, left, pieces, scratch, initial, finish):
    seconds, panel, sems = scratch
    where = Where(place)
    rows = row_copies(start, count, left, panel, sems)
    for copy in rows:
        copy.start()
    gather_second(where, groups, pieces, seconds)
    for i in range(count):
        panel[i, 16, 0] = jnp.zeros(BLOCK, jnp.bfloat16)
    for i in range(count):
        rows[i].wait()
        low = reach[start + i, 0]
        high = reach[start + i, 1]
        flat = panel.at[i].reshape(34, 128, 128)
        acc = row_sum(where, groups, start + i, low, high, pieces, seconds, flat, initial(i))
        live0 = (where.first >= -low) & (where.first <= high)
        live1 = where.first + 16 <= high
        finish(where, i, acc, live0, live1)


def no_sum(i):
    return jnp.zeros((128, 256), jnp.float32)


def in_groups(groups, refs):
    count = 2 * len(groups)
    return [refs[n : n + 2] for n in range(0, count, 2)], refs[count:]


def square_kernel(start, count, groups, place, reach, left, *refs):
    pieces, refs = in_groups(groups, refs)
    if start == 0:
        refs[3][pl.ds(count, count)] = refs[0][...]
        refs = refs[1:]
    (first, second, err), scratch = refs[:3], refs[3:]
    eye = (
        lax.broadcasted_iota(jnp.int32, BLOCK, 0) == lax.broadcasted_iota(jnp.int32, BLOCK, 1)
    ).astype(jnp.float32)

    def finish(where, i, acc, live0, live1):
        total0 = jnp.where(live0, acc[:, :128], 0.0)
        total1 = jnp.where(live1, acc[:, 128:], 0.0)
        first[i] = total0.astype(jnp.bfloat16)
        second[i] = total1.astype(jnp.bfloat16)
        deviation = total0 - jnp.where(live0 & (where.first == 0), 1.0, 0.0) * eye
        squares = deviation * deviation + total1 * total1
        err[i] = jnp.sum(squares.reshape(8, 16, 128), axis=0)

    product_rows(start, count, groups, place, reach, left, pieces, scratch, no_sum, finish)


def early_kernel(groups, place, reach, left, *refs):
    pieces, refs = in_groups(groups, refs)
    out, scratch = refs[0], refs[1:]

    def finish(where, i, acc, live0, live1):
        out[i] = acc

    product_rows(0, 8, groups, place, reach, left, pieces, scratch, no_sum, finish)


def late_kernel(groups, place, reach, left, early, own, parts, *refs):
    pieces, refs = in_groups(groups, refs)
    (out, err), scratch = refs[:2], refs[2:]
    squares = jnp.sum(jnp.sum(parts[...], axis=0), axis=1)
    total = jnp.sum(squares, axis=1, keepdims=True)
    err[...] = jnp.broadcast_to(jnp.sqrt(total / 128), (8, 128))

    def finish(where, i, acc, live0, live1):
        for w, live in enumerate((live0, live1)):
            updated = 1.5 * own[i, w].astype(jnp.float32) - 0.5 * acc[:, 128 * w : 128 * w + 128]
            out[i, w] = jnp.where(live, updated, 0.0).astype(jnp.bfloat16)

    product_rows(0, 8, groups, place, reach, left, pieces, scratch, lambda i: early[i], finish)


SMEM = pl.BlockSpec(memory_space=pltpu.SMEM)
VMEM = pl.BlockSpec(memory_space=pltpu.VMEM)
ANY = pl.BlockSpec(memory_space=pl.ANY)


def call(kernel, name, outs, count, groups, args):
    steps = 4 * count * len(groups)
    return pl.pallas_call(
        functools.partial(kernel, groups),
        out_shape=outs,
        in_specs=[SMEM, SMEM, ANY] + [VMEM] * (len(args) - 3),
        out_specs=jax.tree.map(lambda _: VMEM, outs),
        scratch_shapes=[
            pltpu.VMEM((32 * len(groups) + 1, 128, 128), jnp.bfloat16),
            pltpu.VMEM((count, 17, 2, 128, 128), jnp.bfloat16),
            pltpu.SemaphoreType.DMA((count,)),
        ],
        compiler_params=pltpu.CompilerParams(vmem_limit_bytes=50 * 2**20),
        cost_estimate=pl.CostEstimate(
            flops=steps * 2**24, bytes_accessed=steps * 2**16, transcendentals=0
        ),
        name=name,
    )(*args)


def bf16(*shape):
    return jax.ShapeDtypeStruct(shape, jnp.bfloat16)


def f32(*shape):
    return jax.ShapeDtypeStruct(shape, jnp.float32)


def square_rows(start, args):
    return call(
        lambda groups, *refs: square_kernel(start, 4, groups, *refs),
        "square",
        (bf16(4, 128, 128), bf16(4, 128, 128), f32(8 - start, 16, 128)),
        4,
        (0, 1, 2, 3),
        args,
    )


def per_device(xblocks, reach):
    row_pos = lax.axis_index("row")
    col_pos = lax.axis_index("col")
    place = jnp.stack([row_pos, col_pos]).astype(jnp.int32)
    offset = (col_pos - row_pos + H) % 16 - H
    two_slots = offset + 16 <= H
    own_offset = offset + 16 * jnp.arange(2, dtype=jnp.int32)[None, :]
    live_mask = (own_offset >= -reach[:, 0:1]) & (own_offset <= reach[:, 1:2])

    left = lax.all_gather(xblocks, "col", axis=0)
    masked = jnp.where(live_mask[:, :, None, None], xblocks, jnp.zeros((), xblocks.dtype))
    other = half_way(masked[4:, 1])
    shard = jnp.concatenate([masked[:, 0], jnp.where(two_slots, masked[:4, 1], other)], axis=0)
    panel = panel_of(shard)
    upper = square_rows(4, (place, reach, left, *sum(panel, [])))
    other = half_way(upper[1])
    lower = square_rows(0, (place, reach, left, *sum(panel, []), upper[2]))
    second = jnp.where(two_slots, lower[1], other)
    panel = panel_of(jnp.concatenate([lower[0], upper[0], second], axis=0))

    parts = lax.all_gather(lower[2], "col", axis=0)

    early = call(
        early_kernel, "early", f32(8, 128, 256), 8, (1, 2), (place, reach, left, *panel[1], *panel[2])
    )
    new_x, row_error = call(
        late_kernel,
        "late",
        (bf16(8, 2, 128, 128), f32(8, 128)),
        8,
        (0, 3),
        (place, reach, left, early, xblocks, parts, *panel[0], *panel[3]),
    )
    return (new_x, row_error[:, 0])


def solution(mesh):
    placed = (P("row", "col", None, None), P("row", None))
    return jax.shard_map(
        per_device,
        mesh=mesh,
        in_specs=placed,
        out_specs=(P("row", "col", None, None), P("row")),
        check_vma=False,
    )
```

```python
import functools

import jax
import jax.numpy as jnp
from jax import lax
from jax.experimental import pallas as pl
from jax.experimental.pallas import tpu as pltpu
from jax.sharding import PartitionSpec as P

H = 11
BLOCK = (128, 128)
NO_LEFT = 32
NO_SECOND = 128
GROUP_SHIFTS = (0, -1, 1, 2)


def core_pairs(step, phase):
    pairs = []
    for y in range(4):
        for x in range(4):
            for col in range(16):
                if col % 2 == phase:
                    target = y * 4 + (x + step) % 4
                else:
                    target = (y + step) % 4 * 4 + x
                pairs.append(((y * 4 + x) * 16 + col, target * 16 + col))
    return pairs


def move(value, pairs):
    return lax.ppermute(value, ("row", "col"), pairs)


def half_way(value):
    pairs = [(r * 16 + c, (r + 8) % 16 * 16 + c) for r in range(16) for c in range(16)]
    return move(value, pairs)


def spread(value, phase):
    return [move(value, core_pairs(step, phase)) for step in (1, -1, 2)]


def panel_of(shard):
    near = spread(shard, 0)
    halves = [jnp.stack([shard, near[0]], axis=0), jnp.stack(near[1:], axis=0)]
    before = [move(half, core_pairs(1, 1)) for half in halves]
    after = [move(half, core_pairs(-1, 1)) for half in halves]
    passed = [move(before[0], core_pairs(1, 1)), move(after[1], core_pairs(-1, 1))]
    return [halves, before, after, passed]


def wrap(offset):
    return ((offset + H + 16) & 15) - H


def table_of(a, b, reach):
    x_major = (b & 1) == 0
    x = a & 3
    y = a >> 2
    m = jnp.arange(16, dtype=jnp.int32) >> 2
    j = jnp.arange(16, dtype=jnp.int32) & 3

    def shift(n):
        return jnp.where(n == 1, -1, n - (n >> 1))

    uu = (jnp.where(x_major, x, y) + shift(j) + 4) & 3
    vv = (jnp.where(x_major, y, x) + shift(m) + 4) & 3
    origin = jnp.where(x_major, 4 * vv + uu, 4 * uu + vv)[None, :]
    slot = (4 * m + uu)[None, :]
    first = wrap(b - a)
    low = reach[:, 0:1]
    high = reach[:, 1:2]
    rows = jnp.arange(8, dtype=jnp.int32)[:, None]
    offset = first - wrap(b - origin)
    two = wrap(b - origin) + 16 <= H
    ahead = offset >= 5
    base = (8 * (4 * m + j))[None, :]
    partner = 8 * jnp.where(x_major, 4 * (3 - m) + j, 4 * m + 3 - j)[None, :]
    k0 = ((a + 16 * rows + offset + 128) >> 4) & 7
    k1 = (k0 + 7) & 7
    other = jnp.where(ahead, offset - 16, offset + 16)

    def left_block(offset, shard):
        held = (offset >= -low) & (offset <= high)
        return jnp.where(held, 2 * shard + ((offset + H) >> 4), NO_LEFT)

    useful = two | (offset < 5)
    fields = [
        left_block(offset, slot),
        jnp.where(useful, left_block(other, slot), NO_LEFT),
        k0,
        jnp.where(two, base + k0, NO_SECOND),
        left_block(offset, origin),
        jnp.where(two & ahead, base + k1, NO_SECOND),
        jnp.where(useful, left_block(other, origin), NO_LEFT),
        jnp.where(two, base, partner + 4),
    ]
    shards = jnp.stack([jnp.broadcast_to(f, (8, 16)) for f in fields], axis=2).reshape(8, 128)
    live0 = (first >= -low) & (first <= high)
    live1 = first + 16 <= high
    flags = jnp.concatenate([live0, live1, live0 & (first == 0)], axis=1).astype(jnp.int32)
    return jnp.concatenate([shards, jnp.pad(flags, ((0, 0), (0, 125)))], axis=0)


def gather_second(table, groups, pieces, seconds):
    for m in groups:
        for j in range(4):
            target = table[0, 8 * (4 * m + j) + 7]
            for k in range(4):
                seconds[target + k] = pieces[groups.index(m)][j // 2][j % 2, 8 + k]
    seconds[NO_SECOND] = jnp.zeros(BLOCK, jnp.bfloat16)


def row_sum(table, groups, row, pieces, seconds, panel, acc):
    for n, m in enumerate(groups):
        for j in range(4):
            piece = pieces[n][j // 2].at[j % 2]
            l0, l1, k0, s0, o0, s1, o1 = (table[row, 8 * (4 * m + j) + f] for f in range(7))
            if len(groups) == 4:
                l0, l1 = o0, o1
            else:
                l0, l1 = (jnp.minimum(l - 8 * (m - n), 8 * len(groups)) for l in (l0, l1))
            ahead = s1 != NO_SECOND
            k1 = (k0 + jnp.where(ahead, 7, 1)) & 7
            upper = jnp.concatenate([piece[k0], seconds[s0]], axis=1)
            scaled = piece[k1] * jnp.where(ahead, 0.0, 1.0).astype(jnp.bfloat16)
            lower = jnp.concatenate([seconds[s1], scaled], axis=1)
            acc += jnp.dot(
                jnp.concatenate([panel[l0], panel[l1]], axis=1),
                jnp.concatenate([upper, lower], axis=0),
                preferred_element_type=jnp.float32,
            )
    return acc


class Rows:
    def __init__(self, left, groups, panel, sems):
        self.left = left
        self.groups = groups
        self.panel = panel
        self.sems = sems
        a = lax.axis_index("row")
        self.x_major = (lax.axis_index("col") & 1) == 0
        self.own = jnp.where(self.x_major, a >> 2, a & 3)

    def copy(self, row, m, along_x):
        place = (self.own + GROUP_SHIFTS[m] + 4) & 3
        shards = self.left.at[place, :, row] if along_x else self.left.at[:, place, row]
        target = self.panel.at[row, pl.ds(4 * self.groups.index(m), 4)]
        return pltpu.make_async_copy(shards, target, self.sems.at[row, m])

    def start(self):
        for along_x in (True, False):

            @pl.when(self.x_major == along_x)
            def _():
                for row in range(8):
                    for m in self.groups:
                        self.copy(row, m, along_x).start()

        for row in range(8):
            self.panel[row, 4 * len(self.groups), 0] = jnp.zeros(BLOCK, jnp.bfloat16)

    def wait(self, begin, end):
        for row in range(begin, end):
            for m in self.groups:
                self.copy(row, m, True).wait()


def product_rows(start, begin, count, groups, table, panel, pieces, seconds, initial, finish):
    for i in range(begin, begin + count):
        row = start + i
        flat = panel.at[i].reshape(2 * panel.shape[1], 128, 128)
        acc = row_sum(table, groups, row, pieces, seconds, flat, initial(i))
        finish(i, acc, table[8 + row, 0] != 0, table[8 + row, 1] != 0)


def no_sum(i):
    return jnp.zeros((128, 256), jnp.float32)


def halves_of(refs):
    return [refs[n : n + 2] for n in range(0, len(refs), 2)]


def square_finish(start, table, first, second, err):
    eye = (
        lax.broadcasted_iota(jnp.int32, BLOCK, 0) == lax.broadcasted_iota(jnp.int32, BLOCK, 1)
    ).astype(jnp.float32)

    def finish(i, acc, live0, live1):
        total0 = jnp.where(live0, acc[:, :128], 0.0)
        total1 = jnp.where(live1, acc[:, 128:], 0.0)
        first[i] = total0.astype(jnp.bfloat16)
        second[i] = total1.astype(jnp.bfloat16)
        deviation = total0 - table[8 + start + i, 2].astype(jnp.float32) * eye
        squares = deviation * deviation + total1 * total1
        err[i] = jnp.sum(squares.reshape(8, 16, 128), axis=0)

    return finish


ALL = (0, 1, 2, 3)
EARLY = (1, 2)
LATE = (0, 3)


def square_kernel(start, source, left, *refs):
    if start == 0:
        upper_err, refs = refs[0], refs[1:]
    pieces, (first, second, err, table, table_sem, seconds, panel, sems) = halves_of(refs[:8]), refs[8:]
    load = pltpu.make_async_copy(source, table, table_sem)
    load.start()
    rows = [
        pltpu.make_async_copy(left.at[:, start + i], panel.at[i, pl.ds(0, 16)], sems.at[i, 0])
        for i in range(4)
    ]
    for i in range(4):
        rows[i].start()
        panel[i, 16, 0] = jnp.zeros(BLOCK, jnp.bfloat16)
    if start == 0:
        err[pl.ds(4, 4)] = upper_err[...]
    load.wait()
    gather_second(table, ALL, pieces, seconds)
    finish = square_finish(start, table, first, second, err)
    for i in range(0, 4, 2):
        for row in rows[i : i + 2]:
            row.wait()
        product_rows(start, i, 2, ALL, table, panel, pieces, seconds, no_sum, finish)


def cube_rows(groups, source, left, pieces, table, table_sem, seconds, panel, sems, initial, finish):
    rows = Rows(left, groups, panel, sems)
    load = pltpu.make_async_copy(source, table, table_sem)
    load.start()
    rows.start()
    load.wait()
    gather_second(table, groups, pieces, seconds)
    for i in range(0, 8, 2):
        rows.wait(i, i + 2)
        product_rows(0, i, 2, groups, table, panel, pieces, seconds, initial, finish)


def early_kernel(source, left, *refs):
    pieces, out, scratch = halves_of(refs[:4]), refs[4], refs[5:]

    def finish(i, acc, live0, live1):
        out[i] = acc

    cube_rows(EARLY, source, left, pieces, *scratch, no_sum, finish)


def late_kernel(source, left, early, own, *refs):
    pieces, out, scratch = halves_of(refs[:4]), refs[4], refs[5:]

    def finish(i, acc, live0, live1):
        for w, live in enumerate((live0, live1)):
            updated = 1.5 * own[i, w].astype(jnp.float32) - 0.5 * acc[:, 128 * w : 128 * w + 128]
            out[i, w] = jnp.where(live, updated, 0.0).astype(jnp.bfloat16)

    cube_rows(LATE, source, left, pieces, *scratch, lambda i: early[i], finish)


VMEM = pl.BlockSpec(memory_space=pltpu.VMEM)
ANY = pl.BlockSpec(memory_space=pl.ANY)


def call(kernel, name, outs, args, part):
    return pl.pallas_call(
        kernel,
        out_shape=outs,
        in_specs=[ANY, ANY] + [VMEM] * (len(args) - 2),
        out_specs=jax.tree.map(lambda _: VMEM, outs),
        scratch_shapes=[
            pltpu.SMEM((16, 128), jnp.int32),
            pltpu.SemaphoreType.DMA,
            pltpu.VMEM((NO_SECOND + 1, 128, 128), jnp.bfloat16),
            pltpu.VMEM(part, jnp.bfloat16),
            pltpu.SemaphoreType.DMA((part[0], 4)),
        ],
        compiler_params=pltpu.CompilerParams(vmem_limit_bytes=46 * 2**20),
        cost_estimate=pl.CostEstimate(flops=2**30, bytes_accessed=2**22, transcendentals=0),
        name=name,
    )(*args)


def bf16(*shape):
    return jax.ShapeDtypeStruct(shape, jnp.bfloat16)


def f32(*shape):
    return jax.ShapeDtypeStruct(shape, jnp.float32)


def per_device(xblocks, reach):
    row_pos = lax.axis_index("row").astype(jnp.int32)
    col_pos = lax.axis_index("col").astype(jnp.int32)
    offset = wrap(col_pos - row_pos)
    two_slots = offset + 16 <= H
    own_offset = offset + 16 * jnp.arange(2, dtype=jnp.int32)[None, :]
    live_mask = (own_offset >= -reach[:, 0:1]) & (own_offset <= reach[:, 1:2])

    left = lax.all_gather(xblocks, "col", axis=0)
    masked = jnp.where(live_mask[:, :, None, None], xblocks, jnp.zeros((), xblocks.dtype))
    other = half_way(masked[4:, 1])
    shard = jnp.concatenate([masked[:, 0], jnp.where(two_slots, masked[:4, 1], other)], axis=0)
    table = table_of(row_pos, col_pos, reach)
    pieces = sum(panel_of(shard), [])
    half = bf16(4, 128, 128)
    part = (4, 17, 2, 128, 128)
    first_high, second_high, err_high = call(
        functools.partial(square_kernel, 4),
        "upper",
        (half, half, f32(4, 16, 128)),
        (table, left, *pieces),
        part,
    )
    other = half_way(second_high)
    first_low, second_low, err = call(
        functools.partial(square_kernel, 0),
        "lower",
        (half, half, f32(8, 16, 128)),
        (table, left, err_high, *pieces),
        part,
    )
    second = jnp.where(two_slots, second_low, other)
    own, before, after, passed = panel_of(jnp.concatenate([first_low, first_high, second], axis=0))
    parts = lax.all_gather(err, "col", axis=0)
    part = (8, 9, 2, 128, 128)
    left = left.reshape(4, 4, 8, 2, 128, 128)
    early = call(
        early_kernel, "early", f32(8, 128, 256), (table, left, *before, *after), part
    )
    row_error = jnp.sqrt(jnp.sum(parts, axis=(0, 2, 3)) / 128)
    new_x = call(
        late_kernel,
        "late",
        bf16(8, 2, 128, 128),
        (table, left, early, xblocks, *own, *passed),
        part,
    )
    return (new_x, row_error)


def solution(mesh):
    placed = (P("row", "col", None, None), P("row", None))
    return jax.shard_map(
        per_device,
        mesh=mesh,
        in_specs=placed,
        out_specs=(P("row", "col", None, None), P("row")),
        check_vma=False,
    )
```

```python
import jax
import jax.numpy as jnp
from jax import lax
from jax.experimental import pallas as pl
from jax.experimental.pallas import tpu as pltpu
from jax.sharding import PartitionSpec as P

H = 11
BLOCK = (128, 128)
NO_LEFT = 32
NO_SECOND = 128
GROUP_SHIFTS = (0, -1, 1, 2)


def core_pairs(step, phase):
    pairs = []
    for y in range(4):
        for x in range(4):
            for col in range(16):
                if col % 2 == phase:
                    target = y * 4 + (x + step) % 4
                else:
                    target = (y + step) % 4 * 4 + x
                pairs.append(((y * 4 + x) * 16 + col, target * 16 + col))
    return pairs


def move(value, pairs):
    return lax.ppermute(value, ("row", "col"), pairs)


def half_way(value):
    pairs = [(r * 16 + c, (r + 8) % 16 * 16 + c) for r in range(16) for c in range(16)]
    return move(value, pairs)


def spread(value, phase):
    return [move(value, core_pairs(step, phase)) for step in (1, -1, 2)]


def panel_of(first, second, two_slots):
    other = half_way(second[4:])
    near = spread(first, 0)
    extra = jnp.where(two_slots, second[:4], other)
    extras = spread(extra, 0)
    shards = [
        jnp.concatenate(pair, axis=0) for pair in zip([first] + near, [extra] + extras, strict=True)
    ]
    halves = [jnp.stack(shards[:2], axis=0), jnp.stack(shards[2:], axis=0)]
    before = [move(half, core_pairs(1, 1)) for half in halves]
    after = [move(half, core_pairs(-1, 1)) for half in halves]
    passed = [move(before[0], core_pairs(1, 1)), move(after[1], core_pairs(-1, 1))]
    return [halves, before, after, passed]


def wrap(offset):
    return ((offset + H + 16) & 15) - H


def table_of(a, b, reach):
    x_major = (b & 1) == 0
    x = a & 3
    y = a >> 2
    m = jnp.arange(16, dtype=jnp.int32) >> 2
    j = jnp.arange(16, dtype=jnp.int32) & 3

    def shift(n):
        return jnp.where(n == 1, -1, n - (n >> 1))

    uu = (jnp.where(x_major, x, y) + shift(j) + 4) & 3
    vv = (jnp.where(x_major, y, x) + shift(m) + 4) & 3
    origin = jnp.where(x_major, 4 * vv + uu, 4 * uu + vv)[None, :]
    slot = (4 * m + uu)[None, :]
    first = wrap(b - a)
    low = reach[:, 0:1]
    high = reach[:, 1:2]
    rows = jnp.arange(8, dtype=jnp.int32)[:, None]
    offset = first - wrap(b - origin)
    two = wrap(b - origin) + 16 <= H
    ahead = offset >= 5
    base = (8 * (4 * m + j))[None, :]
    partner = 8 * jnp.where(x_major, 4 * (3 - m) + j, 4 * m + 3 - j)[None, :]
    k0 = ((a + 16 * rows + offset + 128) >> 4) & 7
    k1 = (k0 + 7) & 7
    other = jnp.where(ahead, offset - 16, offset + 16)

    def left_block(offset, shard):
        held = (offset >= -low) & (offset <= high)
        return jnp.where(held, 2 * shard + ((offset + H) >> 4), NO_LEFT)

    useful = two | (offset < 5)
    fields = [
        left_block(offset, slot),
        jnp.where(useful, left_block(other, slot), NO_LEFT),
        k0,
        jnp.where(two, base + k0, NO_SECOND),
        left_block(offset, origin),
        jnp.where(two & ahead, base + k1, NO_SECOND),
        jnp.where(useful, left_block(other, origin), NO_LEFT),
        jnp.where(two, base, partner + 4),
    ]
    shards = jnp.stack([jnp.broadcast_to(f, (8, 16)) for f in fields], axis=2).reshape(8, 128)
    live0 = (first >= -low) & (first <= high)
    live1 = first + 16 <= high
    flags = jnp.concatenate([live0, live1, live0 & (first == 0)], axis=1).astype(jnp.int32)
    return jnp.concatenate([shards, jnp.pad(flags, ((0, 0), (0, 125)))], axis=0)


def gather_second(table, groups, pieces, seconds):
    for m in groups:
        for j in range(4):
            target = table[0, 8 * (4 * m + j) + 7]
            for k in range(4):
                seconds[target + k] = pieces[groups.index(m)][j // 2][j % 2, 8 + k]
    seconds[NO_SECOND] = jnp.zeros(BLOCK, jnp.bfloat16)


def row_sum(table, groups, row, pieces, seconds, panel, acc):
    for n, m in enumerate(groups):
        for j in range(4):
            piece = pieces[n][j // 2].at[j % 2]
            l0, l1, k0, s0, o0, s1, o1 = (table[row, 8 * (4 * m + j) + f] for f in range(7))
            if len(groups) == 4:
                l0, l1 = o0, o1
            else:
                l0, l1 = (jnp.minimum(l - 8 * (m - n), 8 * len(groups)) for l in (l0, l1))
            ahead = s1 != NO_SECOND
            k1 = (k0 + jnp.where(ahead, 7, 1)) & 7
            upper = jnp.concatenate([piece[k0], seconds[s0]], axis=1)
            scaled = piece[k1] * jnp.where(ahead, 0.0, 1.0).astype(jnp.bfloat16)
            lower = jnp.concatenate([seconds[s1], scaled], axis=1)
            acc += jnp.dot(
                jnp.concatenate([panel[l0], panel[l1]], axis=1),
                jnp.concatenate([upper, lower], axis=0),
                preferred_element_type=jnp.float32,
            )
    return acc


class Rows:
    def __init__(self, left, groups, panel, sems):
        self.left = left
        self.groups = groups
        self.panel = panel
        self.sems = sems
        a = lax.axis_index("row")
        self.x_major = (lax.axis_index("col") & 1) == 0
        self.own = jnp.where(self.x_major, a >> 2, a & 3)

    def copy(self, row, m, along_x):
        place = (self.own + GROUP_SHIFTS[m] + 4) & 3
        shards = self.left.at[place, :, row] if along_x else self.left.at[:, place, row]
        target = self.panel.at[row, pl.ds(4 * self.groups.index(m), 4)]
        return pltpu.make_async_copy(shards, target, self.sems.at[row, m])

    def start(self):
        for along_x in (True, False):

            @pl.when(self.x_major == along_x)
            def _():
                @pl.loop(0, 8)
                def _(row):
                    for m in self.groups:
                        self.copy(row, m, along_x).start()

        @pl.loop(0, 8)
        def _(row):
            self.panel[row, 4 * len(self.groups), 0] = jnp.zeros(BLOCK, jnp.bfloat16)

    def wait(self, row):
        for m in self.groups:
            self.copy(row, m, True).wait()


def product_rows(begin, groups, table, panel, pieces, seconds, initial, finish):
    for i in range(2):
        row = begin + i
        flat = panel.at[row].reshape(2 * panel.shape[1], 128, 128)
        acc = row_sum(table, groups, row, pieces, seconds, flat, initial(row))
        finish(row, acc, table[8 + row, 0] != 0, table[8 + row, 1] != 0)


def no_sum(i):
    return jnp.zeros((128, 256), jnp.float32)


def halves_of(refs):
    return [refs[n : n + 2] for n in range(0, len(refs), 2)]


ALL = (0, 1, 2, 3)
EARLY = (1, 2)
LATE = (0, 3)


def square_kernel(source, left, *refs):
    pieces, (first, second, err, table, table_sem, seconds, panel, sems) = halves_of(refs[:8]), refs[8:]
    load = pltpu.make_async_copy(source, table, table_sem)
    load.start()

    def copy(row):
        return pltpu.make_async_copy(left.at[:, row], panel.at[row, pl.ds(0, 16)], sems.at[row, 0])

    @pl.loop(0, 8)
    def _(row):
        copy(row).start()
        panel[row, 16, 0] = jnp.zeros(BLOCK, jnp.bfloat16)

    eye = (
        lax.broadcasted_iota(jnp.int32, BLOCK, 0) == lax.broadcasted_iota(jnp.int32, BLOCK, 1)
    ).astype(jnp.float32)

    def finish(i, acc, live0, live1):
        total0 = jnp.where(live0, acc[:, :128], 0.0)
        total1 = jnp.where(live1, acc[:, 128:], 0.0)
        first[i] = total0.astype(jnp.bfloat16)
        second[i] = total1.astype(jnp.bfloat16)
        deviation = total0 - table[8 + i, 2].astype(jnp.float32) * eye
        squares = deviation * deviation + total1 * total1
        err[i, pl.ds(0, 1)] = jnp.sum(squares, axis=0, keepdims=True)

    err[...] = jnp.zeros(err.shape, jnp.float32)
    load.wait()
    gather_second(table, ALL, pieces, seconds)

    @pl.loop(0, 4)
    def _(n):
        copy(2 * n).wait()
        copy(2 * n + 1).wait()
        product_rows(2 * n, ALL, table, panel, pieces, seconds, no_sum, finish)


def cube_rows(groups, source, left, pieces, table, table_sem, seconds, panel, sems, initial, finish):
    rows = Rows(left, groups, panel, sems)
    load = pltpu.make_async_copy(source, table, table_sem)
    load.start()
    rows.start()
    load.wait()
    gather_second(table, groups, pieces, seconds)

    @pl.loop(0, 4)
    def _(n):
        rows.wait(2 * n)
        rows.wait(2 * n + 1)
        product_rows(2 * n, groups, table, panel, pieces, seconds, initial, finish)


def early_kernel(source, left, *refs):
    pieces, out, scratch = halves_of(refs[:4]), refs[4], refs[5:]

    def finish(i, acc, live0, live1):
        out[i] = acc

    cube_rows(EARLY, source, left, pieces, *scratch, no_sum, finish)


def late_kernel(source, left, early, own, _, *refs):
    pieces, out, scratch = halves_of(refs[:4]), refs[4], refs[5:]

    def finish(i, acc, live0, live1):
        for w, live in enumerate((live0, live1)):
            updated = 1.5 * own[i, w].astype(jnp.float32) - 0.5 * acc[:, 128 * w : 128 * w + 128]
            out[i, w] = jnp.where(live, updated, 0.0).astype(jnp.bfloat16)

    cube_rows(LATE, source, left, pieces, *scratch, lambda i: early[i], finish)


VMEM = pl.BlockSpec(memory_space=pltpu.VMEM)
ANY = pl.BlockSpec(memory_space=pl.ANY)


def call(kernel, name, outs, args, part):
    return pl.pallas_call(
        kernel,
        out_shape=outs,
        in_specs=[ANY, ANY] + [VMEM] * (len(args) - 2),
        out_specs=jax.tree.map(lambda _: VMEM, outs),
        scratch_shapes=[
            pltpu.SMEM((16, 128), jnp.int32),
            pltpu.SemaphoreType.DMA,
            pltpu.VMEM((NO_SECOND + 1, 128, 128), jnp.bfloat16),
            pltpu.VMEM(part, jnp.bfloat16),
            pltpu.SemaphoreType.DMA((part[0], 4)),
        ],
        compiler_params=pltpu.CompilerParams(vmem_limit_bytes=46 * 2**20),
        cost_estimate=pl.CostEstimate(flops=2**30, bytes_accessed=2**22, transcendentals=0),
        name=name,
    )(*args)


def bf16(*shape):
    return jax.ShapeDtypeStruct(shape, jnp.bfloat16)


def f32(*shape):
    return jax.ShapeDtypeStruct(shape, jnp.float32)


def per_device(xblocks, reach):
    row_pos = lax.axis_index("row").astype(jnp.int32)
    col_pos = lax.axis_index("col").astype(jnp.int32)
    offset = wrap(col_pos - row_pos)
    two_slots = offset + 16 <= H
    own_offset = offset + 16 * jnp.arange(2, dtype=jnp.int32)[None, :]
    live_mask = (own_offset >= -reach[:, 0:1]) & (own_offset <= reach[:, 1:2])

    left = lax.all_gather(xblocks, "col", axis=0)
    masked = jnp.where(live_mask[:, :, None, None], xblocks, jnp.zeros((), xblocks.dtype))
    table = table_of(row_pos, col_pos, reach)
    pieces = sum(panel_of(masked[:, 0], masked[:, 1], two_slots), [])
    half = bf16(8, 128, 128)
    first, second, err = call(
        square_kernel,
        "square",
        (half, half, f32(8, 16, 128)),
        (table, left, *pieces),
        (8, 17, 2, 128, 128),
    )
    own, before, after, passed = panel_of(first, second, two_slots)
    parts = lax.all_gather(err, "col", axis=0)
    part = (8, 9, 2, 128, 128)
    left = left.reshape(4, 4, 8, 2, 128, 128)
    early = call(
        early_kernel, "early", f32(8, 128, 256), (table, left, *before, *after), part
    )
    row_error = jnp.sqrt(jnp.sum(parts[:, :, 0], axis=(0, 2)) / 128)
    new_x = call(
        late_kernel,
        "late",
        bf16(8, 2, 128, 128),
        (table, left, early, xblocks, row_error, *own, *passed),
        part,
    )
    return (new_x, row_error)


def solution(mesh):
    placed = (P("row", "col", None, None), P("row", None))
    return jax.shard_map(
        per_device,
        mesh=mesh,
        in_specs=placed,
        out_specs=(P("row", "col", None, None), P("row")),
        check_vma=False,
    )
```

```python
import jax
import jax.numpy as jnp
from jax import lax
from jax.experimental import pallas as pl
from jax.experimental.pallas import tpu as pltpu
from jax.sharding import PartitionSpec as P

H = 11
BLOCK = (128, 128)
NO_LEFT = 32
NO_SECOND = 128
GROUP_SHIFTS = (0, -1, 1, 2)


def core_pairs(step, phase):
    pairs = []
    for y in range(4):
        for x in range(4):
            for col in range(16):
                if col % 2 == phase:
                    target = y * 4 + (x + step) % 4
                else:
                    target = (y + step) % 4 * 4 + x
                pairs.append(((y * 4 + x) * 16 + col, target * 16 + col))
    return pairs


def move(value, pairs):
    return lax.ppermute(value, ("row", "col"), pairs)


def half_way(value):
    pairs = [(r * 16 + c, (r + 8) % 16 * 16 + c) for r in range(16) for c in range(16)]
    return move(value, pairs)


def panel_of(first, second, two_slots):
    other = half_way(second[4:])
    near = [move(first, core_pairs(step, 0)) for step in (1, -1)]
    extra = jnp.where(two_slots, second[:4], other)
    extras = [move(extra, core_pairs(step, 0)) for step in (1, -1)]
    shard = jnp.concatenate([first, extra], axis=0)
    shards = [shard] + [
        jnp.concatenate(pair, axis=0) for pair in zip(near, extras, strict=True)
    ]
    shards.append(move(shard, core_pairs(2, 0)))
    halves = [jnp.stack(shards[:2], axis=0), jnp.stack(shards[2:], axis=0)]
    before = [move(half, core_pairs(1, 1)) for half in halves]
    after = [move(half, core_pairs(-1, 1)) for half in halves]
    passed = [move(before[0], core_pairs(1, 1)), move(after[1], core_pairs(-1, 1))]
    return [halves, before, after, passed]


def wrap(offset):
    return ((offset + H + 16) & 15) - H


def table_of(a, b, reach):
    x_major = (b & 1) == 0
    x = a & 3
    y = a >> 2
    m = jnp.arange(16, dtype=jnp.int32) >> 2
    j = jnp.arange(16, dtype=jnp.int32) & 3

    def shift(n):
        return jnp.where(n == 1, -1, n - (n >> 1))

    uu = (jnp.where(x_major, x, y) + shift(j) + 4) & 3
    vv = (jnp.where(x_major, y, x) + shift(m) + 4) & 3
    origin = jnp.where(x_major, 4 * vv + uu, 4 * uu + vv)[None, :]
    slot = (4 * m + uu)[None, :]
    first = wrap(b - a)
    low = reach[:, 0:1]
    high = reach[:, 1:2]
    rows = jnp.arange(8, dtype=jnp.int32)[:, None]
    offset = first - wrap(b - origin)
    two = wrap(b - origin) + 16 <= H
    ahead = offset >= 5
    base = (8 * (4 * m + j))[None, :]
    partner = 8 * jnp.where(x_major, 4 * (3 - m) + j, 4 * m + 3 - j)[None, :]
    k0 = ((a + 16 * rows + offset + 128) >> 4) & 7
    k1 = (k0 + 7) & 7
    other = jnp.where(ahead, offset - 16, offset + 16)

    def left_block(offset, shard):
        held = (offset >= -low) & (offset <= high)
        return jnp.where(held, 2 * shard + ((offset + H) >> 4), NO_LEFT)

    useful = two | (offset < 5)
    fields = [
        left_block(offset, slot),
        jnp.where(useful, left_block(other, slot), NO_LEFT),
        k0,
        jnp.where(two, base + k0, NO_SECOND),
        left_block(offset, origin),
        jnp.where(two & ahead, base + k1, NO_SECOND),
        jnp.where(useful, left_block(other, origin), NO_LEFT),
        jnp.where(two, base, partner + 4),
    ]
    shards = jnp.stack([jnp.broadcast_to(f, (8, 16)) for f in fields], axis=2).reshape(8, 128)
    live0 = (first >= -low) & (first <= high)
    live1 = first + 16 <= high
    flags = jnp.concatenate([live0, live1, live0 & (first == 0)], axis=1).astype(jnp.int32)
    return jnp.concatenate([shards, jnp.pad(flags, ((0, 0), (0, 125)))], axis=0)


def gather_second(table, groups, pieces, seconds):
    for m in groups:
        for j in range(4):
            target = table[0, 8 * (4 * m + j) + 7]
            for k in range(4):
                seconds[target + k] = pieces[groups.index(m)][j // 2][j % 2, 8 + k]
    seconds[NO_SECOND] = jnp.zeros(BLOCK, jnp.bfloat16)


def row_sum(table, groups, row, pieces, seconds, panel, acc):
    for n, m in enumerate(groups):
        for j in range(4):
            piece = pieces[n][j // 2].at[j % 2]
            l0, l1, k0, s0, o0, s1, o1 = (table[row, 8 * (4 * m + j) + f] for f in range(7))
            if len(groups) == 4:
                l0, l1 = o0, o1
            else:
                l0, l1 = (jnp.minimum(l - 8 * (m - n), 8 * len(groups)) for l in (l0, l1))
            ahead = s1 != NO_SECOND
            k1 = (k0 + jnp.where(ahead, 7, 1)) & 7
            upper = jnp.concatenate([piece[k0], seconds[s0]], axis=1)
            scaled = piece[k1] * jnp.where(ahead, 0.0, 1.0).astype(jnp.bfloat16)
            lower = jnp.concatenate([seconds[s1], scaled], axis=1)
            acc += jnp.dot(
                jnp.concatenate([panel[l0], panel[l1]], axis=1),
                jnp.concatenate([upper, lower], axis=0),
                preferred_element_type=jnp.float32,
            )
    return acc


class Rows:
    def __init__(self, left, groups, panel, sems):
        self.left = left
        self.groups = groups
        self.panel = panel
        self.sems = sems
        a = lax.axis_index("row")
        self.x_major = (lax.axis_index("col") & 1) == 0
        self.own = jnp.where(self.x_major, a >> 2, a & 3)

    def copy(self, row, m, along_x):
        place = (self.own + GROUP_SHIFTS[m] + 4) & 3
        shards = self.left.at[place, :, row] if along_x else self.left.at[:, place, row]
        target = self.panel.at[row, pl.ds(4 * self.groups.index(m), 4)]
        return pltpu.make_async_copy(shards, target, self.sems.at[row, m])

    def start(self):
        for along_x in (True, False):

            @pl.when(self.x_major == along_x)
            def _():
                @pl.loop(0, 8)
                def _(row):
                    for m in self.groups:
                        self.copy(row, m, along_x).start()

        @pl.loop(0, 8)
        def _(row):
            self.panel[row, 4 * len(self.groups), 0] = jnp.zeros(BLOCK, jnp.bfloat16)

    def wait(self, row):
        for m in self.groups:
            self.copy(row, m, True).wait()


def product_rows(begin, groups, table, panel, pieces, seconds, initial, finish):
    for i in range(2):
        row = begin + i
        flat = panel.at[row].reshape(2 * panel.shape[1], 128, 128)
        acc = row_sum(table, groups, row, pieces, seconds, flat, initial(row))
        finish(row, acc, table[8 + row, 0] != 0, table[8 + row, 1] != 0)


def no_sum(i):
    return jnp.zeros((128, 256), jnp.float32)


def halves_of(refs):
    return [refs[n : n + 2] for n in range(0, len(refs), 2)]


ALL = (0, 1, 2, 3)
EARLY = (1, 2)
LATE = (0, 3)


def square_kernel(source, left, *refs):
    pieces, (first, second, err, table, table_sem, seconds, panel, sems) = halves_of(refs[:8]), refs[8:]
    load = pltpu.make_async_copy(source, table, table_sem)
    load.start()

    def copy(row):
        return pltpu.make_async_copy(left.at[:, row], panel.at[row, pl.ds(0, 16)], sems.at[row, 0])

    @pl.loop(0, 8)
    def _(row):
        copy(row).start()
        panel[row, 16, 0] = jnp.zeros(BLOCK, jnp.bfloat16)

    eye = (
        lax.broadcasted_iota(jnp.int32, BLOCK, 0) == lax.broadcasted_iota(jnp.int32, BLOCK, 1)
    ).astype(jnp.float32)

    def finish(i, acc, live0, live1):
        total0 = jnp.where(live0, acc[:, :128], 0.0)
        total1 = jnp.where(live1, acc[:, 128:], 0.0)
        first[i] = total0.astype(jnp.bfloat16)
        second[i] = total1.astype(jnp.bfloat16)
        deviation = total0 - table[8 + i, 2].astype(jnp.float32) * eye
        squares = deviation * deviation + total1 * total1
        err[i, pl.ds(0, 1)] = jnp.sum(squares, axis=0, keepdims=True)

    err[...] = jnp.zeros(err.shape, jnp.float32)
    load.wait()
    gather_second(table, ALL, pieces, seconds)

    @pl.loop(0, 4)
    def _(n):
        copy(2 * n).wait()
        copy(2 * n + 1).wait()
        product_rows(2 * n, ALL, table, panel, pieces, seconds, no_sum, finish)


def cube_rows(groups, source, left, pieces, table, table_sem, seconds, panel, sems, initial, finish):
    rows = Rows(left, groups, panel, sems)
    load = pltpu.make_async_copy(source, table, table_sem)
    load.start()
    rows.start()
    load.wait()
    gather_second(table, groups, pieces, seconds)

    @pl.loop(0, 4)
    def _(n):
        rows.wait(2 * n)
        rows.wait(2 * n + 1)
        product_rows(2 * n, groups, table, panel, pieces, seconds, initial, finish)


def early_kernel(source, left, *refs):
    pieces, out, scratch = halves_of(refs[:4]), refs[4], refs[5:]

    def finish(i, acc, live0, live1):
        out[i] = acc

    cube_rows(EARLY, source, left, pieces, *scratch, no_sum, finish)


def late_kernel(source, left, early, own, _, *refs):
    pieces, out, scratch = halves_of(refs[:4]), refs[4], refs[5:]

    def finish(i, acc, live0, live1):
        for w, live in enumerate((live0, live1)):
            updated = 1.5 * own[i, w].astype(jnp.float32) - 0.5 * acc[:, 128 * w : 128 * w + 128]
            out[i, w] = jnp.where(live, updated, 0.0).astype(jnp.bfloat16)

    cube_rows(LATE, source, left, pieces, *scratch, lambda i: early[i], finish)


VMEM = pl.BlockSpec(memory_space=pltpu.VMEM)
ANY = pl.BlockSpec(memory_space=pl.ANY)


def call(kernel, name, outs, args, part):
    return pl.pallas_call(
        kernel,
        out_shape=outs,
        in_specs=[ANY, ANY] + [VMEM] * (len(args) - 2),
        out_specs=jax.tree.map(lambda _: VMEM, outs),
        scratch_shapes=[
            pltpu.SMEM((16, 128), jnp.int32),
            pltpu.SemaphoreType.DMA,
            pltpu.VMEM((NO_SECOND + 1, 128, 128), jnp.bfloat16),
            pltpu.VMEM(part, jnp.bfloat16),
            pltpu.SemaphoreType.DMA((part[0], 4)),
        ],
        compiler_params=pltpu.CompilerParams(vmem_limit_bytes=46 * 2**20),
        cost_estimate=pl.CostEstimate(flops=2**30, bytes_accessed=2**22, transcendentals=0),
        name=name,
    )(*args)


def bf16(*shape):
    return jax.ShapeDtypeStruct(shape, jnp.bfloat16)


def f32(*shape):
    return jax.ShapeDtypeStruct(shape, jnp.float32)


def per_device(xblocks, reach):
    row_pos = lax.axis_index("row").astype(jnp.int32)
    col_pos = lax.axis_index("col").astype(jnp.int32)
    offset = wrap(col_pos - row_pos)
    two_slots = offset + 16 <= H
    own_offset = offset + 16 * jnp.arange(2, dtype=jnp.int32)[None, :]
    live_mask = (own_offset >= -reach[:, 0:1]) & (own_offset <= reach[:, 1:2])

    left = lax.all_gather(xblocks, "col", axis=0)
    masked = jnp.where(live_mask[:, :, None, None], xblocks, jnp.zeros((), xblocks.dtype))
    table = table_of(row_pos, col_pos, reach)
    pieces = sum(panel_of(masked[:, 0], masked[:, 1], two_slots), [])
    half = bf16(8, 128, 128)
    first, second, err = call(
        square_kernel,
        "square",
        (half, half, f32(8, 16, 128)),
        (table, left, *pieces),
        (8, 17, 2, 128, 128),
    )
    own, before, after, passed = panel_of(first, second, two_slots)
    parts = lax.all_gather(err, "col", axis=0)
    part = (8, 9, 2, 128, 128)
    left = left.reshape(4, 4, 8, 2, 128, 128)
    early = call(
        early_kernel, "early", f32(8, 128, 256), (table, left, *before, *after), part
    )
    row_error = jnp.sqrt(jnp.sum(parts[:, :, 0], axis=(0, 2)) / 128)
    new_x = call(
        late_kernel,
        "late",
        bf16(8, 2, 128, 128),
        (table, left, early, xblocks, row_error, *own, *passed),
        part,
    )
    return (new_x, row_error)


def solution(mesh):
    placed = (P("row", "col", None, None), P("row", None))
    return jax.shard_map(
        per_device,
        mesh=mesh,
        in_specs=placed,
        out_specs=(P("row", "col", None, None), P("row")),
        check_vma=False,
    )
```

```python
import jax
import jax.numpy as jnp
from jax import lax
from jax.experimental import pallas as pl
from jax.experimental.pallas import tpu as pltpu
from jax.sharding import PartitionSpec as P

H = 11
BLOCK = (128, 128)
NO_LEFT = 32
NO_SECOND = 128
GROUP_SHIFTS = (0, -1, 1, 2)


def core_pairs(step, phase):
    pairs = []
    for y in range(4):
        for x in range(4):
            for col in range(16):
                if col % 2 == phase:
                    target = y * 4 + (x + step) % 4
                else:
                    target = (y + step) % 4 * 4 + x
                pairs.append(((y * 4 + x) * 16 + col, target * 16 + col))
    return pairs


def move(value, pairs):
    return lax.ppermute(value, ("row", "col"), pairs)


def half_way(value):
    pairs = [(r * 16 + c, (r + 8) % 16 * 16 + c) for r in range(16) for c in range(16)]
    return move(value, pairs)


def spread(value, phase):
    return [move(value, core_pairs(step, phase)) for step in (1, -1, 2)]


def panel_of(first, second, two_slots):
    other = half_way(second[4:])
    near = spread(first, 0)
    extra = jnp.where(two_slots, second[:4], other)
    extras = spread(extra, 0)
    shards = [
        jnp.concatenate(pair, axis=0) for pair in zip([first] + near, [extra] + extras, strict=True)
    ]
    halves = [jnp.stack(shards[:2], axis=0), jnp.stack(shards[2:], axis=0)]
    before = [move(half, core_pairs(1, 1)) for half in halves]
    after = [move(half, core_pairs(-1, 1)) for half in halves]
    passed = [move(before[0], core_pairs(1, 1)), move(after[1], core_pairs(-1, 1))]
    return [halves, before, after, passed]


def wrap(offset):
    return ((offset + H + 16) & 15) - H


def table_of(a, b, reach):
    x_major = (b & 1) == 0
    x = a & 3
    y = a >> 2
    m = jnp.arange(16, dtype=jnp.int32) >> 2
    j = jnp.arange(16, dtype=jnp.int32) & 3

    def shift(n):
        return jnp.where(n == 1, -1, n - (n >> 1))

    uu = (jnp.where(x_major, x, y) + shift(j) + 4) & 3
    vv = (jnp.where(x_major, y, x) + shift(m) + 4) & 3
    origin = jnp.where(x_major, 4 * vv + uu, 4 * uu + vv)[None, :]
    slot = (4 * m + uu)[None, :]
    first = wrap(b - a)
    low = reach[:, 0:1]
    high = reach[:, 1:2]
    rows = jnp.arange(8, dtype=jnp.int32)[:, None]
    offset = first - wrap(b - origin)
    two = wrap(b - origin) + 16 <= H
    ahead = offset >= 5
    base = (8 * (4 * m + j))[None, :]
    partner = 8 * jnp.where(x_major, 4 * (3 - m) + j, 4 * m + 3 - j)[None, :]
    k0 = ((a + 16 * rows + offset + 128) >> 4) & 7
    k1 = (k0 + 7) & 7
    other = jnp.where(ahead, offset - 16, offset + 16)

    def left_block(offset, shard):
        held = (offset >= -low) & (offset <= high)
        return jnp.where(held, 2 * shard + ((offset + H) >> 4), NO_LEFT)

    useful = two | (offset < 5)
    fields = [
        left_block(offset, slot),
        jnp.where(useful, left_block(other, slot), NO_LEFT),
        k0,
        jnp.where(two, base + k0, NO_SECOND),
        left_block(offset, origin),
        jnp.where(two & ahead, base + k1, NO_SECOND),
        jnp.where(useful, left_block(other, origin), NO_LEFT),
        jnp.where(two, base, partner + 4),
    ]
    shards = jnp.stack([jnp.broadcast_to(f, (8, 16)) for f in fields], axis=2).reshape(8, 128)
    live0 = (first >= -low) & (first <= high)
    live1 = first + 16 <= high
    flags = jnp.concatenate([live0, live1, live0 & (first == 0)], axis=1).astype(jnp.int32)
    return jnp.concatenate([shards, jnp.pad(flags, ((0, 0), (0, 125)))], axis=0)


def gather_second(table, groups, pieces, seconds):
    for m in groups:
        for j in range(4):
            target = table[0, 8 * (4 * m + j) + 7]
            for k in range(4):
                seconds[target + k] = pieces[groups.index(m)][j // 2][j % 2, 8 + k]
    seconds[NO_SECOND] = jnp.zeros(BLOCK, jnp.bfloat16)


def row_sum(table, groups, row, pieces, seconds, panel, acc):
    for n, m in enumerate(groups):
        for j in range(4):
            piece = pieces[n][j // 2].at[j % 2]
            l0, l1, k0, s0, o0, s1, o1 = (table[row, 8 * (4 * m + j) + f] for f in range(7))
            if len(groups) == 4:
                l0, l1 = o0, o1
            else:
                l0, l1 = (jnp.minimum(l - 8 * (m - n), 8 * len(groups)) for l in (l0, l1))
            ahead = s1 != NO_SECOND
            k1 = (k0 + jnp.where(ahead, 7, 1)) & 7
            upper = jnp.concatenate([piece[k0], seconds[s0]], axis=1)
            scaled = piece[k1] * jnp.where(ahead, 0.0, 1.0).astype(jnp.bfloat16)
            lower = jnp.concatenate([seconds[s1], scaled], axis=1)
            acc += jnp.dot(
                jnp.concatenate([panel[l0], panel[l1]], axis=1),
                jnp.concatenate([upper, lower], axis=0),
                preferred_element_type=jnp.float32,
            )
    return acc


class Rows:
    def __init__(self, left, groups, panel, sems):
        self.left = left
        self.groups = groups
        self.panel = panel
        self.sems = sems
        a = lax.axis_index("row")
        self.x_major = (lax.axis_index("col") & 1) == 0
        self.own = jnp.where(self.x_major, a >> 2, a & 3)

    def copy(self, row, m, along_x):
        place = (self.own + GROUP_SHIFTS[m] + 4) & 3
        shards = self.left.at[place, :, row] if along_x else self.left.at[:, place, row]
        target = self.panel.at[row, pl.ds(4 * self.groups.index(m), 4)]
        return pltpu.make_async_copy(shards, target, self.sems.at[row, m])

    def start(self):
        for along_x in (True, False):

            @pl.when(self.x_major == along_x)
            def _():
                @pl.loop(0, 8)
                def _(row):
                    for m in self.groups:
                        self.copy(row, m, along_x).start()

        @pl.loop(0, 8)
        def _(row):
            self.panel[row, 4 * len(self.groups), 0] = jnp.zeros(BLOCK, jnp.bfloat16)

    def wait(self, row):
        for m in self.groups:
            self.copy(row, m, True).wait()


def product_rows(begin, groups, table, panel, pieces, seconds, initial, finish):
    for i in range(2):
        row = begin + i
        flat = panel.at[row].reshape(2 * panel.shape[1], 128, 128)
        acc = row_sum(table, groups, row, pieces, seconds, flat, initial(row))
        finish(row, acc, table[8 + row, 0] != 0, table[8 + row, 1] != 0)


def no_sum(i):
    return jnp.zeros((128, 256), jnp.float32)


def halves_of(refs):
    return [refs[n : n + 2] for n in range(0, len(refs), 2)]


ALL = (0, 1, 2, 3)
EARLY = (1, 2)
LATE = (0, 3)


def square_kernel(source, left, *refs):
    pieces, (first, second, err, table, table_sem, seconds, panel, sems) = halves_of(refs[:8]), refs[8:]
    load = pltpu.make_async_copy(source, table, table_sem)
    load.start()

    def copy(row):
        return pltpu.make_async_copy(left.at[:, row], panel.at[row, pl.ds(0, 16)], sems.at[row, 0])

    @pl.loop(0, 8)
    def _(row):
        copy(row).start()
        panel[row, 16, 0] = jnp.zeros(BLOCK, jnp.bfloat16)

    eye = (
        lax.broadcasted_iota(jnp.int32, BLOCK, 0) == lax.broadcasted_iota(jnp.int32, BLOCK, 1)
    ).astype(jnp.float32)

    def finish(i, acc, live0, live1):
        total0 = jnp.where(live0, acc[:, :128], 0.0)
        total1 = jnp.where(live1, acc[:, 128:], 0.0)
        first[i] = total0.astype(jnp.bfloat16)
        second[i] = total1.astype(jnp.bfloat16)
        deviation = total0 - table[8 + i, 2].astype(jnp.float32) * eye
        squares = deviation * deviation + total1 * total1
        err[i, pl.ds(0, 1)] = jnp.sum(squares, axis=0, keepdims=True)

    err[...] = jnp.zeros(err.shape, jnp.float32)
    load.wait()
    gather_second(table, ALL, pieces, seconds)

    @pl.loop(0, 4)
    def _(n):
        copy(2 * n).wait()
        copy(2 * n + 1).wait()
        product_rows(2 * n, ALL, table, panel, pieces, seconds, no_sum, finish)


def cube_rows(groups, source, left, pieces, table, table_sem, seconds, panel, sems, initial, finish):
    rows = Rows(left, groups, panel, sems)
    load = pltpu.make_async_copy(source, table, table_sem)
    load.start()
    rows.start()
    load.wait()
    gather_second(table, groups, pieces, seconds)

    @pl.loop(0, 4)
    def _(n):
        rows.wait(2 * n)
        rows.wait(2 * n + 1)
        product_rows(2 * n, groups, table, panel, pieces, seconds, initial, finish)


def early_kernel(source, left, *refs):
    pieces, out, scratch = halves_of(refs[:4]), refs[4], refs[5:]

    def finish(i, acc, live0, live1):
        out[i] = acc

    cube_rows(EARLY, source, left, pieces, *scratch, no_sum, finish)


def late_kernel(source, left, early, own, _, *refs):
    pieces, out, scratch = halves_of(refs[:4]), refs[4], refs[5:]

    def finish(i, acc, live0, live1):
        for w, live in enumerate((live0, live1)):
            updated = 1.5 * own[i, w].astype(jnp.float32) - 0.5 * acc[:, 128 * w : 128 * w + 128]
            out[i, w] = jnp.where(live, updated, 0.0).astype(jnp.bfloat16)

    cube_rows(LATE, source, left, pieces, *scratch, lambda i: early[i], finish)


VMEM = pl.BlockSpec(memory_space=pltpu.VMEM)
ANY = pl.BlockSpec(memory_space=pl.ANY)


def call(kernel, name, outs, args, part):
    return pl.pallas_call(
        kernel,
        out_shape=outs,
        in_specs=[ANY if n < 2 or arg.ndim == 1 else VMEM for n, arg in enumerate(args)],
        out_specs=jax.tree.map(lambda _: VMEM, outs),
        scratch_shapes=[
            pltpu.SMEM((16, 128), jnp.int32),
            pltpu.SemaphoreType.DMA,
            pltpu.VMEM((NO_SECOND + 1, 128, 128), jnp.bfloat16),
            pltpu.VMEM(part, jnp.bfloat16),
            pltpu.SemaphoreType.DMA((part[0], 4)),
        ],
        compiler_params=pltpu.CompilerParams(vmem_limit_bytes=46 * 2**20),
        cost_estimate=pl.CostEstimate(flops=2**30, bytes_accessed=2**22, transcendentals=0),
        name=name,
    )(*args)


def bf16(*shape):
    return jax.ShapeDtypeStruct(shape, jnp.bfloat16)


def f32(*shape):
    return jax.ShapeDtypeStruct(shape, jnp.float32)


def per_device(xblocks, reach):
    row_pos = lax.axis_index("row").astype(jnp.int32)
    col_pos = lax.axis_index("col").astype(jnp.int32)
    offset = wrap(col_pos - row_pos)
    two_slots = offset + 16 <= H
    own_offset = offset + 16 * jnp.arange(2, dtype=jnp.int32)[None, :]
    live_mask = (own_offset >= -reach[:, 0:1]) & (own_offset <= reach[:, 1:2])

    left = lax.all_gather(xblocks, "col", axis=0)
    masked = jnp.where(live_mask[:, :, None, None], xblocks, jnp.zeros((), xblocks.dtype))
    table = table_of(row_pos, col_pos, reach)
    pieces = sum(panel_of(masked[:, 0], masked[:, 1], two_slots), [])
    half = bf16(8, 128, 128)
    first, second, err = call(
        square_kernel,
        "square",
        (half, half, f32(8, 16, 128)),
        (table, left, *pieces),
        (8, 17, 2, 128, 128),
    )
    own, before, after, passed = panel_of(first, second, two_slots)
    parts = lax.all_gather(err, "col", axis=0)
    part = (8, 9, 2, 128, 128)
    left = left.reshape(4, 4, 8, 2, 128, 128)
    early = call(
        early_kernel, "early", f32(8, 128, 256), (table, left, *before, *after), part
    )
    row_error = jnp.sqrt(jnp.sum(parts[:, :, 0], axis=(0, 2)) / 128)
    new_x = call(
        late_kernel,
        "late",
        bf16(8, 2, 128, 128),
        (table, left, early, xblocks, row_error, *own, *passed),
        part,
    )
    return (new_x, row_error)


def solution(mesh):
    placed = (P("row", "col", None, None), P("row", None))
    return jax.shard_map(
        per_device,
        mesh=mesh,
        in_specs=placed,
        out_specs=(P("row", "col", None, None), P("row")),
        check_vma=False,
    )
```
